512 devices in a mesh: dp: 64 (over z, y), seq: 8 (over x, core).
Axes of the slice: x: 4, y: 8, z: 8, core: 2. Of those that a mesh axis runs over, the one named last changes fastest.
Arguments:
- queries: bfloat16 [512, 152, 4096], P(('dp', 'seq')), may hold values from -120 to 120
- candidate_keys: bfloat16 [512, 152, 1024], P(('dp', 'seq')), may hold values from -5 to 5
- candidate_values: bfloat16 [512, 152, 1024], P(('dp', 'seq')), may hold values from -6 to 6
- grad_output: bfloat16 [512, 152, 4096], P(('dp', 'seq')), may hold values from -24 to 24
- prefix_keys: bfloat16 [64, 56, 1024], P('dp', None, 'seq'), may hold values from -6 to 6
- prefix_values: bfloat16 [64, 56, 1024], P('dp', None, 'seq'), may hold values from -6 to 6
- query_index: int32 [512], replicated, may hold values from 0 to 63
- candidate_length: int32 [512], replicated, may hold values from 1 to 152, as said below
- prefix_length: int32 [64], replicated, may hold values from 1 to 56, as said below
Outputs:
- grad_queries: bfloat16 [512, 152, 4096], P(('dp', 'seq'))
- grad_candidate_keys: bfloat16 [512, 152, 1024], P(('dp', 'seq'))
- grad_candidate_values: bfloat16 [512, 152, 1024], P(('dp', 'seq'))
- grad_prefix_keys: float32 [64, 56, 1024], P('dp', None, 'seq')
- grad_prefix_values: float32 [64, 56, 1024], P('dp', None, 'seq')
The draws below stay inside these ranges and needn't reach their ends.
Inputs may be any that keep to these rules, and one draw needn't show every extreme that they name: `candidate_length`: some candidate has all 152 tokens live. `prefix_length`: some query has all 56 prefix tokens live.
All inputs are finite; a program needn't handle non-finite values.
Results may differ from the reference program's by a relative error of at most 0.02.
Values may be sent and summed in bfloat16 or wider, within the bound.
No kernel may reach another device: no remote copies, remote signals or barrier semaphores. Data moves between devices by JAX's collectives and lax.ppermute only.
A program may use at most 64 MiB of HBM per device.

```python
import math
import jax
import jax.numpy as jnp
import numpy as np
from jax import lax

H = 32
KVH = 8
HD = 128
CLEN = 152
PLEN = 56
NQ = 64
CANDS = 512


def shared_rows(key):
    base = jnp.clip(jax.random.normal(jax.random.fold_in(key, 11), (CANDS, CLEN, KVH * HD), jnp.float32), -5.0, 5.0)
    return base


def draw_candidate_keys(key, part):
    base = shared_rows(key)
    return base.astype(jnp.bfloat16)


def draw_queries(key, part):
    key = jax.random.fold_in(key, 2)
    return jnp.clip(jax.random.normal(key, (CANDS, CLEN, H * HD), jnp.float32), -5.0, 5.0).astype(jnp.bfloat16)


def draw_candidate_length(key, part):
    key = jax.random.fold_in(key, 4)
    lengths = jax.random.randint(key, (CANDS,), 1, CLEN + 1)
    spot = jax.random.randint(jax.random.fold_in(key, 5), (), 0, CANDS)
    return jnp.where(jnp.arange(CANDS) == spot, CLEN, lengths).astype(jnp.int32)


def draw_prefix_length(key, part):
    key = jax.random.fold_in(key, 6)
    lengths = jax.random.randint(key, (NQ,), 1, PLEN + 1)
    spot = jax.random.randint(jax.random.fold_in(key, 7), (), 0, NQ)
    return jnp.where(jnp.arange(NQ) == spot, PLEN, lengths).astype(jnp.int32)


def place_ends(entries, key, smallest, high):
    longest = entries.shape.index(max(entries.shape))
    spots = []
    for shift in (0, 1):
        where = [jax.random.randint(jax.random.fold_in(key, axis), (), 0, length) for axis, length in enumerate(entries.shape)]
        where[longest] = (where[longest] + shift) % entries.shape[longest]
        spots.append(tuple(where))
    return entries.at[spots[0]].set(smallest).at[spots[1]].set(high)


def shard_levels(stream_key, extent, split, low, high):
    def one(dim, parts):
        heights = jax.random.uniform(jax.random.fold_in(jax.random.fold_in(stream_key, 6), dim), (parts,), jnp.float32, low / len(split), high / len(split))
        return jnp.repeat(jnp.exp(heights), extent[dim] // parts).reshape((-1,) + (1,) * (len(extent) - dim - 1))

    level = one(*split[0])
    for cut in split[1:]:
        level = level * one(*cut)
    return level


def rank_table(amount, lean):
    portions = [(1 << 20) // math.isqrt(rank ** lean) + 1 for rank in range(1, amount + 1)]
    deviation = 1 + sum(portions) // (1 << 30)
    return np.cumsum(np.array([max(1, weight // deviation) for weight in portions]))


def ranked_ids(own_key, dims, number_of, skew):
    grid = rank_table(number_of, skew)
    ticket = jax.random.randint(jax.random.fold_in(own_key, 1), dims, 0, int(grid[number_of - 1]))
    rank = jnp.searchsorted(jnp.asarray(grid, jnp.int32), ticket, side="right")
    return jax.random.permutation(jax.random.fold_in(own_key, 2), number_of)[rank].astype(jnp.int32)


def normal_values(rng, extent, scale, bound, cuts=(), held_as=jnp.bfloat16):
    array = scale * jax.random.normal(rng, extent, jnp.float32)
    if cuts:
        array = array * shard_levels(rng, extent, cuts, -0.22, 0.18)
    return jnp.clip(array, -bound, bound).astype(held_as)


def setup_inputs(seed: int = 0) -> dict:
    seeds = jax.random.split(jax.random.key(seed), 10)
    return {
        "queries": draw_queries(jax.random.fold_in(seeds[9], 71), 0),
        "candidate_keys": draw_candidate_keys(jax.random.fold_in(seeds[9], 71), 0),
        "candidate_values": normal_values(seeds[2], (CANDS, CLEN, KVH * HD), 1.0, 6.0, ((0, 512),)),
        "grad_output": normal_values(seeds[3], (CANDS, CLEN, H * HD), 4.0, 24.0, ((0, 512),)),
        "prefix_keys": normal_values(seeds[4], (NQ, PLEN, KVH * HD), 1.0, 6.0, ((0, 64), (2, 8))),
        "prefix_values": normal_values(seeds[5], (NQ, PLEN, KVH * HD), 1.0, 6.0, ((0, 64), (2, 8))),
        "query_index": place_ends(ranked_ids(seeds[6], (CANDS,), NQ, 1), jax.random.fold_in(seeds[6], 3), 0, NQ - 1).astype(jnp.int32),
        "candidate_length": draw_candidate_length(jax.random.fold_in(seeds[9], 71), 0),
        "prefix_length": draw_prefix_length(jax.random.fold_in(seeds[9], 71), 0),
    }


def attend(queries, keys_in, values_in, grad_output, prefix_keys, prefix_values, lengths, prefix_lengths):
    count, rows, width_q = queries.shape
    prefix_rows = prefix_keys.shape[1]
    kv_heads = keys_in.shape[2] // HD
    group = width_q // (kv_heads * HD)
    span = prefix_rows + rows
    scale = 1.0 / math.sqrt(HD)
    all_keys = jnp.concatenate([prefix_keys, keys_in], axis=1).reshape(count, span, kv_heads, HD).astype(jnp.float32)
    all_values = jnp.concatenate([prefix_values, values_in], axis=1).reshape(count, span, kv_heads, HD).astype(jnp.float32)
    query_heads = queries.reshape(count, rows, kv_heads, group, HD).astype(jnp.float32)
    position = jnp.arange(rows)[None, :, None]
    column = jnp.arange(span)[None, None, :]
    inside = column - prefix_rows
    allowed = jnp.where(column < prefix_rows, column < prefix_lengths[:, None, None], jnp.logical_and(inside <= position, inside < lengths[:, None, None]))
    allowed = allowed[:, None, None]
    scores = jnp.einsum('ctgrd,cugd->cgrtu', query_heads, all_keys, precision=lax.Precision.HIGHEST) * scale
    scores = jnp.where(allowed, scores, -1e+30)
    highest = lax.optimization_barrier(jnp.max(scores, axis=-1, keepdims=True))
    expon = jnp.where(allowed, jnp.exp(scores - highest), 0.0)
    probs = expon / lax.optimization_barrier(jnp.sum(expon, axis=-1, keepdims=True))
    probs_low = probs.astype(jnp.bfloat16).astype(jnp.float32)
    live = jnp.arange(rows)[None, :] < lengths[:, None]
    masked_grad = jnp.where(live[:, :, None], grad_output, jnp.zeros((), grad_output.dtype))
    grad_heads = masked_grad.reshape(count, rows, kv_heads, group, HD).astype(jnp.float32)
    attended = jnp.einsum('cgrtu,cugd->ctgrd', probs_low, all_values, precision=lax.Precision.HIGHEST)
    delta = jnp.moveaxis(lax.optimization_barrier(jnp.sum(grad_heads * attended, axis=-1)), 1, 3)
    value_terms = jnp.einsum('cgrtu,ctgrd->cugd', probs_low, grad_heads, precision=lax.Precision.HIGHEST)
    grad_probs = jnp.einsum('ctgrd,cugd->cgrtu', grad_heads, all_values, precision=lax.Precision.HIGHEST)
    grad_scores = (probs * (grad_probs - delta[..., None]) * scale).astype(jnp.bfloat16).astype(jnp.float32)
    query_grads = jnp.einsum('cgrtu,cugd->ctgrd', grad_scores, all_keys, precision=lax.Precision.HIGHEST)
    query_grads = query_grads.astype(jnp.bfloat16).reshape(count, rows, width_q)
    key_terms = jnp.einsum('cgrtu,ctgrd->cugd', grad_scores, query_heads, precision=lax.Precision.HIGHEST)
    key_terms = key_terms.reshape(count, span, kv_heads * HD)
    value_terms = value_terms.reshape(count, span, kv_heads * HD)
    return (query_grads, key_terms[:, prefix_rows:].astype(jnp.bfloat16), value_terms[:, prefix_rows:].astype(jnp.bfloat16), key_terms[:, :prefix_rows], value_terms[:, :prefix_rows])

def reference(queries, candidate_keys, candidate_values, grad_output, prefix_keys, prefix_values, query_index, candidate_length, prefix_length):
    own_prefix = prefix_length[query_index]

    def single(items):
        query_rows, key_rows, value_rows, grad_rows, owner, length, prefix = items
        owner_keys = lax.dynamic_index_in_dim(prefix_keys, owner.astype(jnp.int32), 0, keepdims=True)
        owner_values = lax.dynamic_index_in_dim(prefix_values, owner.astype(jnp.int32), 0, keepdims=True)
        results = attend(query_rows[None], key_rows[None], value_rows[None], grad_rows[None], owner_keys, owner_values, length[None], prefix[None])
        return tuple((part[0] for part in results))
    query_grads, key_grads, value_grads, key_terms, value_terms = lax.map(single, (queries, candidate_keys, candidate_values, grad_output, query_index, candidate_length, own_prefix))
    prefix_key_grads = jax.ops.segment_sum(key_terms, query_index, num_segments=NQ)
    prefix_value_grads = jax.ops.segment_sum(value_terms, query_index, num_segments=NQ)
    return (query_grads, key_grads, value_grads, prefix_key_grads, prefix_value_grads)
```

```python
import functools
import math

import jax
import jax.numpy as jnp
from jax import lax
from jax.experimental import pallas as pl
from jax.experimental.pallas import tpu as pltpu
from jax.sharding import Mesh, PartitionSpec as P

HD = 128
PAD = 16
NEG = -1e30
VMEM = 48 * 1024 * 1024


def stack_heads(ref, out, rows, group, stride):
    for h in range(group):
        out[pl.ds(h * stride, rows), :] = ref[0, :, h * HD : (h + 1) * HD]


def dot_nt(a, b):
    return lax.dot_general(a, b, (((1,), (1,)), ((), ())), preferred_element_type=jnp.float32)


def dot_nn(a, b):
    return lax.dot_general(a, b, (((1,), (0,)), ((), ())), preferred_element_type=jnp.float32)


def dot_tn(a, b):
    return lax.dot_general(a, b, (((0,), (0,)), ((), ())), preferred_element_type=jnp.float32)


def own_bias(bias, length, rows, group, stride):
    inside = lax.broadcasted_iota(jnp.int32, (rows, stride), 0)
    row = lax.broadcasted_iota(jnp.int32, (rows, stride), 1)
    tile = jnp.where(jnp.logical_and(inside <= row, inside < length), 0.0, NEG)
    bias[...] = jnp.concatenate([tile] * group, axis=1)


def prologue(q4, g4):
    q4[...] = jnp.zeros_like(q4)
    g4[...] = jnp.zeros_like(g4)


def own_stats(dims, meta, q, g, k, v, stats, q4, g4, bias):
    rows, group, stride, factor, _ = dims

    @pl.when(pl.program_id(0) == 0)
    def _():
        prologue(q4, g4)
        own_bias(bias, meta[0], rows, group, stride)

    stack_heads(q, q4, rows, group, stride)
    stack_heads(g, g4, rows, group, stride)
    scores = dot_nt(k[0], q4[...]) * factor + bias[...]
    highest = jnp.max(scores, axis=0, keepdims=True)
    expon = jnp.exp2(scores - highest)
    grad_probs = dot_nt(v[0], g4[...])
    stats[0, 0:1, :] = highest
    stats[0, 1:2, :] = jnp.sum(expon, axis=0, keepdims=True)
    stats[0, 2:3, :] = jnp.sum(expon * grad_probs, axis=0, keepdims=True)


def live_lanes(length, group, stride):
    row = lax.broadcasted_iota(jnp.int32, (1, stride), 1)
    live = jnp.where(row < length, 1.0, 0.0)
    return jnp.concatenate([live] * group, axis=1)


def prefix_bias(prefix_length, prefix_rows, width):
    column = lax.broadcasted_iota(jnp.int32, (prefix_rows, width), 0)
    return jnp.where(column < prefix_length, 0.0, NEG)


def prefix_terms(dims, meta, q, g, stats, pair, total, terms, q4, g4):
    rows, group, stride, factor, scale = dims
    prefix_rows = pair.shape[1]

    @pl.when(pl.program_id(0) == 0)
    def _():
        prologue(q4, g4)

    stack_heads(q, q4, rows, group, stride)
    stack_heads(g, g4, rows, group, stride)
    keys = pair[0, :, 0:HD]
    values = pair[0, :, HD : 2 * HD]
    scores = dot_nt(keys, q4[...]) * factor + prefix_bias(meta[1], prefix_rows, group * stride)
    own_high = stats[0, 0:1, :]
    highest = jnp.maximum(own_high, jnp.max(scores, axis=0, keepdims=True))
    expon = jnp.exp2(scores - highest)
    fade = jnp.exp2(own_high - highest)
    weight = fade * stats[0, 1:2, :] + jnp.sum(expon, axis=0, keepdims=True)
    inverse = live_lanes(meta[0], group, stride) / weight
    grad_probs = dot_nt(values, g4[...])
    delta = fade * stats[0, 2:3, :] + jnp.sum(expon * grad_probs, axis=0, keepdims=True)
    delta = delta * inverse
    probs = expon * inverse
    grad_scores = (probs * (grad_probs - delta) * scale).astype(jnp.bfloat16)
    total[0, 0:1, :] = highest
    total[0, 1:2, :] = inverse
    total[0, 2:3, :] = delta
    key_terms = dot_nn(grad_scores, q4[...])
    value_terms = dot_nn(probs.astype(jnp.bfloat16), g4[...])
    for side in range(terms.shape[0]):
        mine = meta[2] == side
        terms[side, 0, :, 0:HD] = jnp.where(mine, key_terms, 0.0).astype(jnp.bfloat16)
        terms[side, 0, :, HD : 2 * HD] = jnp.where(mine, value_terms, 0.0).astype(jnp.bfloat16)


def own_grads(dims, meta, q, g, k, v, total, pair, dq, dk, dv, q4, g4, bias):
    rows, group, stride, factor, scale = dims
    prefix_rows = pair.shape[1]

    @pl.when(pl.program_id(0) == 0)
    def _():
        prologue(q4, g4)
        own_bias(bias, meta[0], rows, group, stride)

    stack_heads(q, q4, rows, group, stride)
    stack_heads(g, g4, rows, group, stride)
    highest = total[0, 0:1, :]
    inverse = total[0, 1:2, :]
    delta = total[0, 2:3, :]

    def one(keys, values, mask):
        scores = dot_nt(keys, q4[...]) * factor + mask
        probs = jnp.exp2(scores - highest) * inverse
        grad_probs = dot_nt(values, g4[...])
        return probs, (probs * (grad_probs - delta) * scale).astype(jnp.bfloat16)

    keys = pair[0, :, 0:HD]
    values = pair[0, :, HD : 2 * HD]
    _, prefix_scores = one(keys, values, prefix_bias(meta[1], prefix_rows, group * stride))
    probs, grad_scores = one(k[0], v[0], bias[...])
    dv[0] = dot_nn(probs.astype(jnp.bfloat16), g4[...]).astype(jnp.bfloat16)
    dk[0] = dot_nn(grad_scores, q4[...]).astype(jnp.bfloat16)
    for h in range(group):
        lanes = slice(h * stride, (h + 1) * stride)
        rows_q = dot_tn(grad_scores[:, lanes], k[0]) + dot_tn(prefix_scores[:, lanes], keys)
        dq[0, :, h * HD : (h + 1) * HD] = rows_q[:rows].astype(jnp.bfloat16)


def pick_rows(index, source, out, sems):
    copies = [
        pltpu.make_async_copy(source.at[index[i]], out.at[i], sems.at[i])
        for i in range(out.shape[0])
    ]
    for copy in copies:
        copy.start()
    for copy in copies:
        copy.wait()


def add_rows(index, source, out, acc):
    acc[...] = jnp.zeros_like(acc)
    for i in range(source.shape[0]):
        at = index[i]
        acc[at] = acc[at] + source[i].astype(jnp.float32)
    out[...] = acc[...].astype(jnp.bfloat16)


def sum_rows(source, keys, values):
    total = source[0].astype(jnp.float32)
    for i in range(1, source.shape[0]):
        total = total + source[i].astype(jnp.float32)
    keys[0] = total[:, 0:HD]
    values[0] = total[:, HD : 2 * HD]


PARAMS = pltpu.CompilerParams(vmem_limit_bytes=VMEM)


def cost(flops, nbytes):
    return pl.CostEstimate(flops=flops, bytes_accessed=nbytes, transcendentals=flops // 256)


def local(
    queries,
    candidate_keys,
    candidate_values,
    grad_output,
    prefix_keys,
    prefix_values,
    query_index,
    candidate_length,
    prefix_length,
):
    far, near, seq = ("zh", "y"), ("zl", "seq"), "seq"
    rows, width_q = queries.shape[1:]
    kv_heads = candidate_keys.shape[2] // HD
    group = width_q // (kv_heads * HD)
    prefix_rows = prefix_keys.shape[1]
    stride = -(-rows // PAD) * PAD
    width = group * stride
    scale = 1.0 / math.sqrt(HD)
    dims = (rows, group, stride, scale * math.log2(math.e), scale)
    size_l, size_y, size_s = (lax.axis_size(a) for a in ("zl", "y", seq))
    size_h = lax.axis_size("zh")
    n_far, n_near = size_h * size_y, size_l * size_s
    zh, zl, y, s = (lax.axis_index(a) for a in ("zh", "zl", "y", seq))

    def place(query):
        z, owner_y = query // size_y, query % size_y
        return (z // size_l) * size_y + owner_y, z % size_l

    side = jnp.arange(size_l, dtype=jnp.int32)
    first = ((zh * size_l + side) * size_y + y) * size_s
    members = (first[:, None] + jnp.arange(size_s, dtype=jnp.int32)[None, :]).reshape(-1)
    member_far, member_zl = place(query_index[members])
    mine = ((zh * size_l + zl) * size_y + y) * size_s + s
    query = query_index[mine]
    _, query_zl = place(query)
    meta = jnp.stack([candidate_length[mine], prefix_length[query], query_zl]).astype(jnp.int32)

    smem = pl.BlockSpec(memory_space=pltpu.SMEM)
    any_space = pl.BlockSpec(memory_space=pl.ANY)
    vmem = pl.BlockSpec(memory_space=pltpu.VMEM)
    heads_q = pl.BlockSpec((1, rows, group * HD), lambda i, m: (0, 0, i))
    heads_k = pl.BlockSpec((1, rows, HD), lambda i, m: (0, 0, i))
    lanes = pl.BlockSpec((1, 8, width), lambda i, m: (i, 0, 0))
    picked = pl.BlockSpec(
        (1, prefix_rows, 2 * HD), lambda i, m: (m[2] * kv_heads + i, 0, 0)
    )
    packed = pltpu.VMEM((width, HD), jnp.bfloat16)
    bias = pltpu.VMEM((rows, width), jnp.float32)
    lane_shape = jax.ShapeDtypeStruct((kv_heads, 8, width), jnp.float32)
    big = kv_heads * width * rows * HD * 2

    own_pair = jnp.concatenate([prefix_keys[0], prefix_values[0]], axis=1)
    everyone = jnp.broadcast_to(own_pair[None], (n_far,) + own_pair.shape)
    held = lax.all_to_all(everyone, far, 0, 0, tiled=True)
    stats = pl.pallas_call(
        functools.partial(own_stats, dims),
        grid_spec=pltpu.PrefetchScalarGridSpec(
            num_scalar_prefetch=1,
            grid=(kv_heads,),
            in_specs=[heads_q, heads_q, heads_k, heads_k],
            out_specs=lanes,
            scratch_shapes=[packed, packed, bias],
        ),
        out_shape=lane_shape,
        compiler_params=PARAMS,
        cost_estimate=cost(2 * big, 3 << 20),
        name="own_stats",
    )(meta, queries, grad_output, candidate_keys, candidate_values)
    chosen = pl.pallas_call(
        pick_rows,
        in_specs=[smem, any_space],
        out_specs=any_space,
        out_shape=jax.ShapeDtypeStruct((n_near,) + own_pair.shape, jnp.bfloat16),
        scratch_shapes=[pltpu.SemaphoreType.DMA((n_near,))],
        compiler_params=PARAMS,
        name="pick_rows",
    )(member_far, held)
    pairs = lax.all_to_all(chosen, near, 0, 0, tiled=True)

    total, terms = pl.pallas_call(
        functools.partial(prefix_terms, dims),
        grid_spec=pltpu.PrefetchScalarGridSpec(
            num_scalar_prefetch=1,
            grid=(kv_heads,),
            in_specs=[heads_q, heads_q, lanes, picked],
            out_specs=[
                lanes,
                pl.BlockSpec((size_l, 1, prefix_rows, 2 * HD), lambda i, m: (0, i, 0, 0)),
            ],
            scratch_shapes=[packed, packed],
        ),
        out_shape=[
            lane_shape,
            jax.ShapeDtypeStruct((size_l, kv_heads, prefix_rows, 2 * HD), jnp.bfloat16),
        ],
        compiler_params=PARAMS,
        cost_estimate=cost(2 * big, 3 << 20),
        name="prefix_terms",
    )(meta, queries, grad_output, stats, pairs)

    returned = lax.all_to_all(
        terms.reshape(n_near, prefix_rows, 2 * HD), near, 0, 0, tiled=True
    )
    summed = pl.pallas_call(
        add_rows,
        in_specs=[smem, vmem],
        out_specs=vmem,
        out_shape=jax.ShapeDtypeStruct((n_far, prefix_rows, 2 * HD), jnp.bfloat16),
        scratch_shapes=[pltpu.VMEM((n_far, prefix_rows, 2 * HD), jnp.float32)],
        compiler_params=PARAMS,
        name="add_rows",
    )(member_far, returned)
    owned = lax.all_to_all(summed, far, 0, 0, tiled=True)
    grad_prefix_keys, grad_prefix_values = pl.pallas_call(
        sum_rows,
        in_specs=[vmem],
        out_specs=[vmem, vmem],
        out_shape=[jax.ShapeDtypeStruct((1, prefix_rows, HD), jnp.float32)] * 2,
        compiler_params=PARAMS,
        name="sum_rows",
    )(owned)

    grad_queries, grad_keys, grad_values = pl.pallas_call(
        functools.partial(own_grads, dims),
        grid_spec=pltpu.PrefetchScalarGridSpec(
            num_scalar_prefetch=1,
            grid=(kv_heads,),
            in_specs=[heads_q, heads_q, heads_k, heads_k, lanes, picked],
            out_specs=[heads_q, heads_k, heads_k],
            scratch_shapes=[packed, packed, bias],
        ),
        out_shape=[
            jax.ShapeDtypeStruct(queries.shape, jnp.bfloat16),
            jax.ShapeDtypeStruct(candidate_keys.shape, jnp.bfloat16),
            jax.ShapeDtypeStruct(candidate_values.shape, jnp.bfloat16),
        ],
        compiler_params=PARAMS,
        cost_estimate=cost(6 * big, 6 << 20),
        name="own_grads",
    )(meta, queries, grad_output, candidate_keys, candidate_values, total, pairs)
    return grad_queries, grad_keys, grad_values, grad_prefix_keys, grad_prefix_values


def solution(mesh, parts=(4, 2, 8)):
    seq = mesh.shape["seq"]
    inner = Mesh(mesh.devices.reshape(parts + (seq,)), ("zh", "zl", "y", "seq"))
    dp = ("zh", "zl", "y")
    both = dp + ("seq",)
    in_specs = (
        P(both, None, None),
        P(both, None, None),
        P(both, None, None),
        P(both, None, None),
        P(dp, None, "seq"),
        P(dp, None, "seq"),
        P(),
        P(),
        P(),
    )
    out_specs = (
        P(both, None, None),
        P(both, None, None),
        P(both, None, None),
        P(dp, None, "seq"),
        P(dp, None, "seq"),
    )
    return jax.shard_map(local, mesh=inner, in_specs=in_specs, out_specs=out_specs, check_vma=False)
```

```python
import functools
import math

import jax
import jax.numpy as jnp
from jax import lax
from jax.experimental import pallas as pl
from jax.experimental.pallas import tpu as pltpu
from jax.sharding import Mesh, PartitionSpec as P

HD = 128
PAD = 16
NEG = -1e30
VMEM = 60 * 1024 * 1024


def stack_heads(ref, out, part, rows, group, stride):
    for h in range(group):
        lanes = slice((part * group + h) * HD, (part * group + h + 1) * HD)
        out[part, pl.ds(h * stride, rows), :] = ref[0, :, lanes]


def dot_nt(a, b):
    return lax.dot_general(a, b, (((1,), (1,)), ((), ())), preferred_element_type=jnp.float32)


def dot_nn(a, b):
    return lax.dot_general(a, b, (((1,), (0,)), ((), ())), preferred_element_type=jnp.float32)


def dot_tn(a, b):
    return lax.dot_general(a, b, (((0,), (0,)), ((), ())), preferred_element_type=jnp.float32)


def own_bias(bias, length, rows, group, stride):
    inside = lax.broadcasted_iota(jnp.int32, (rows, stride), 0)
    row = lax.broadcasted_iota(jnp.int32, (rows, stride), 1)
    tile = jnp.where(jnp.logical_and(inside <= row, inside < length), 0.0, NEG)
    bias[...] = jnp.concatenate([tile] * group, axis=1)


def prologue(q4, g4):
    q4[...] = jnp.zeros_like(q4)
    g4[...] = jnp.zeros_like(g4)


def own_stats(dims, skips, where, index, lengths, prefixes, q, g, k, v, *refs):
    meta, members, stats, q4, g4, bias = refs
    rows, group, stride, factor, _ = dims

    @pl.when(pl.program_id(0) == 0)
    def _():
        length = lengths[where[1]]
        meta[0] = length
        meta[1] = prefixes[index[where[1]]]
        for i, skip in enumerate(skips):
            members[i] = index[where[0] + skip]
        prologue(q4, g4)
        own_bias(bias, length, rows, group, stride)

    for part in range(q4.shape[0]):
        stack_heads(q, q4, part, rows, group, stride)
        stack_heads(g, g4, part, rows, group, stride)
        lanes = slice(part * HD, (part + 1) * HD)
        scores = dot_nt(k[0, :, lanes], q4[part]) * factor + bias[...]
        highest = jnp.max(scores, axis=0, keepdims=True)
        expon = jnp.exp2(scores - highest)
        grad_probs = dot_nt(v[0, :, lanes], g4[part])
        stats[part, 0:1, :] = highest
        stats[part, 1:2, :] = jnp.sum(expon, axis=0, keepdims=True)
        stats[part, 2:3, :] = jnp.sum(expon * grad_probs, axis=0, keepdims=True)


def live_lanes(length, group, stride):
    row = lax.broadcasted_iota(jnp.int32, (1, stride), 1)
    live = jnp.where(row < length, 1.0, 0.0)
    return jnp.concatenate([live] * group, axis=1)


def prefix_bias(prefix_length, prefix_rows, width):
    column = lax.broadcasted_iota(jnp.int32, (prefix_rows, width), 0)
    return jnp.where(column < prefix_length, 0.0, NEG)


def prefix_terms(dims, meta, q, g, stats, pair, total, terms, q4, g4):
    rows, group, stride, factor, scale = dims
    half = pair.shape[0] // 2
    prefix_rows = half * pair.shape[2]

    @pl.when(pl.program_id(0) == 0)
    def _():
        prologue(q4, g4)

    mask = prefix_bias(meta[1], prefix_rows, group * stride)
    live = live_lanes(meta[0], group, stride)
    for part in range(q4.shape[0]):
        stack_heads(q, q4, part, rows, group, stride)
        stack_heads(g, g4, part, rows, group, stride)
        keys = pair[0:half, part].reshape(prefix_rows, HD)
        values = pair[half:, part].reshape(prefix_rows, HD)
        scores = dot_nt(keys, q4[part]) * factor + mask
        own_high = stats[part, 0:1, :]
        highest = jnp.maximum(own_high, jnp.max(scores, axis=0, keepdims=True))
        expon = jnp.exp2(scores - highest)
        fade = jnp.exp2(own_high - highest)
        weight = fade * stats[part, 1:2, :] + jnp.sum(expon, axis=0, keepdims=True)
        inverse = live / weight
        grad_probs = dot_nt(values, g4[part])
        delta = fade * stats[part, 2:3, :] + jnp.sum(expon * grad_probs, axis=0, keepdims=True)
        delta = delta * inverse
        probs = expon * inverse
        grad_scores = (probs * (grad_probs - delta) * scale).astype(jnp.bfloat16)
        total[part, 0:1, :] = highest
        total[part, 1:2, :] = inverse
        total[part, 2:3, :] = delta
        key_terms = dot_nn(grad_scores, q4[part])
        value_terms = dot_nn(probs.astype(jnp.bfloat16), g4[part])
        terms[0:half, part] = key_terms.astype(jnp.bfloat16).reshape((half,) + terms.shape[2:])
        terms[half:, part] = value_terms.astype(jnp.bfloat16).reshape((half,) + terms.shape[2:])


def own_grads(dims, meta, q, g, k, v, total, pair, dq, dk, dv, q4, g4, bias):
    rows, group, stride, factor, scale = dims
    half = pair.shape[0] // 2
    prefix_rows = half * pair.shape[2]

    @pl.when(pl.program_id(0) == 0)
    def _():
        prologue(q4, g4)
        own_bias(bias, meta[0], rows, group, stride)

    prefix_mask = prefix_bias(meta[1], prefix_rows, group * stride)
    for part in range(q4.shape[0]):
        stack_heads(q, q4, part, rows, group, stride)
        stack_heads(g, g4, part, rows, group, stride)
        highest = total[part, 0:1, :]
        inverse = total[part, 1:2, :]
        delta = total[part, 2:3, :]

        def one(keys, values, mask):
            scores = dot_nt(keys, q4[part]) * factor + mask
            probs = jnp.exp2(scores - highest) * inverse
            grad_probs = dot_nt(values, g4[part])
            return probs, (probs * (grad_probs - delta) * scale).astype(jnp.bfloat16)

        keys = pair[0:half, part].reshape(prefix_rows, HD)
        values = pair[half:, part].reshape(prefix_rows, HD)
        here = slice(part * HD, (part + 1) * HD)
        _, prefix_scores = one(keys, values, prefix_mask)
        probs, grad_scores = one(k[0, :, here], v[0, :, here], bias[...])
        dv[0, :, here] = dot_nn(probs.astype(jnp.bfloat16), g4[part]).astype(jnp.bfloat16)
        dk[0, :, here] = dot_nn(grad_scores, q4[part]).astype(jnp.bfloat16)
        for h in range(group):
            lanes = slice(h * stride, (h + 1) * stride)
            rows_q = dot_tn(grad_scores[:, lanes], k[0, :, here])
            rows_q = rows_q + dot_tn(prefix_scores[:, lanes], keys)
            at = part * group + h
            dq[0, :, at * HD : (at + 1) * HD] = rows_q[:rows].astype(jnp.bfloat16)


def spread(places, keys, values, out, whole):
    prefix_rows = keys.shape[1]
    piece = out.shape[1]
    whole[...] = jnp.zeros_like(whole)
    whole[0:prefix_rows, :] = keys[0]
    middle = whole.shape[0] // 2
    whole[middle : middle + prefix_rows, :] = values[0]
    for i, place in enumerate(places):
        out[i] = whole[place * piece : (place + 1) * piece, :]


def pick_rows(members, source, out):
    for i in range(out.shape[0]):
        out[i] = source[members[i]]


def add_rows(members, source, out, acc):
    acc[...] = jnp.zeros_like(acc)
    for i in range(source.shape[0]):
        at = members[i]
        acc[at] = acc[at] + source[i].astype(jnp.float32)
    out[...] = acc[...].astype(jnp.bfloat16)


def sum_rows(places, source, keys, values):
    piece = source.shape[1]
    count = max(places) + 1
    totals = [None] * count
    for i, place in enumerate(places):
        row = source[i].astype(jnp.float32)
        totals[place] = row if totals[place] is None else totals[place] + row
    for place, total in enumerate(totals):
        out = keys if place < count // 2 else values
        at = (place % (count // 2)) * piece
        size = max(0, min(piece, out.shape[1] - at))
        if size:
            out[0, at : at + size, :] = total[:size]


PARAMS = pltpu.CompilerParams(vmem_limit_bytes=VMEM)


def cost(flops, nbytes):
    return pl.CostEstimate(flops=flops, bytes_accessed=nbytes, transcendentals=flops // 256)


def local(
    queries,
    candidate_keys,
    candidate_values,
    grad_output,
    prefix_keys,
    prefix_values,
    query_index,
    candidate_length,
    prefix_length,
):
    far, near, seq = ("zh", "zl", "yh", "yl"), ("zl", "yl", "seq"), "seq"
    rows, width_q = queries.shape[1:]
    kv_heads = candidate_keys.shape[2] // HD
    group = width_q // (kv_heads * HD)
    prefix_rows = prefix_keys.shape[1]
    stride = -(-rows // PAD) * PAD
    width = group * stride
    scale = 1.0 / math.sqrt(HD)
    dims = (rows, group, stride, scale * math.log2(math.e), scale)
    sizes = tuple(lax.axis_size(a) for a in far)
    size_zh, size_zl, size_yh, size_yl = sizes
    size_s = lax.axis_size(seq)
    pieces = size_zl * size_yl
    n_far, n_near = size_zh * size_zl * size_yh * size_yl, pieces * size_s
    half = pieces // 2
    piece = -(-prefix_rows // (half * PAD)) * PAD
    places = tuple(
        ((i // (size_yl * size_yh)) % size_zl) * size_yl + i % size_yl for i in range(n_far)
    )
    skips = tuple(
        (zl * size_yh * size_yl + yl) * size_s + s
        for zl in range(size_zl)
        for yl in range(size_yl)
        for s in range(size_s)
    )
    zh, zl, yh, yl, s = (lax.axis_index(a) for a in far + (seq,))
    first = (zh * size_zl * size_yh + yh) * size_yl * size_s
    mine = first + (zl * size_yh * size_yl + yl) * size_s + s
    where = jnp.stack([first, mine]).astype(jnp.int32)

    smem = pl.BlockSpec(memory_space=pltpu.SMEM)
    vmem = pl.BlockSpec(memory_space=pltpu.VMEM)
    per = 2 if kv_heads % 2 == 0 else 1
    steps = kv_heads // per
    per = 2 if kv_heads % 2 == 0 else 1
    steps = kv_heads // per
    heads_q = pl.BlockSpec((1, rows, per * group * HD), lambda i: (0, 0, i))
    heads_k = pl.BlockSpec((1, rows, per * HD), lambda i: (0, 0, i))
    lanes = pl.BlockSpec((per, 8, width), lambda i: (i, 0, 0))
    parted = pl.BlockSpec((pieces, per, piece, HD), lambda i: (0, i, 0, 0))
    packed = pltpu.VMEM((per, width, HD), jnp.bfloat16)
    bias = pltpu.VMEM((rows, width), jnp.float32)
    lane_shape = jax.ShapeDtypeStruct((kv_heads, 8, width), jnp.float32)
    far_shape = (n_far, piece, HD)
    near_shape = (n_near, piece, HD)
    part_shape = (pieces, kv_heads, piece, HD)
    big = kv_heads * width * rows * HD * 2

    everyone = pl.pallas_call(
        functools.partial(spread, places),
        in_specs=[vmem, vmem],
        out_specs=vmem,
        out_shape=jax.ShapeDtypeStruct(far_shape, jnp.bfloat16),
        scratch_shapes=[pltpu.VMEM((pieces * piece, HD), jnp.bfloat16)],
        compiler_params=PARAMS,
        name="spread",
    )(prefix_keys, prefix_values)
    held = lax.all_to_all(everyone, far, 0, 0, tiled=True)
    meta, members, stats = pl.pallas_call(
        functools.partial(own_stats, dims, skips),
        grid=(steps,),
        in_specs=[smem, smem, smem, smem, heads_q, heads_q, heads_k, heads_k],
        out_specs=[smem, smem, lanes],
        scratch_shapes=[packed, packed, bias],
        out_shape=[
            jax.ShapeDtypeStruct((2,), jnp.int32),
            jax.ShapeDtypeStruct((n_near,), jnp.int32),
            lane_shape,
        ],
        compiler_params=PARAMS,
        cost_estimate=cost(2 * big, 3 << 20),
        name="own_stats",
    )(
        where,
        query_index,
        candidate_length,
        prefix_length,
        queries,
        grad_output,
        candidate_keys,
        candidate_values,
    )
    chosen = pl.pallas_call(
        pick_rows,
        in_specs=[smem, vmem],
        out_specs=vmem,
        out_shape=jax.ShapeDtypeStruct(near_shape, jnp.bfloat16),
        compiler_params=PARAMS,
        name="pick_rows",
    )(members, held)
    pairs = lax.all_to_all(chosen, near, 0, 0, tiled=True).reshape(part_shape)

    total, terms = pl.pallas_call(
        functools.partial(prefix_terms, dims),
        grid=(steps,),
        in_specs=[smem, heads_q, heads_q, lanes, parted],
        out_specs=[lanes, parted],
        scratch_shapes=[packed, packed],
        out_shape=[lane_shape, jax.ShapeDtypeStruct(part_shape, jnp.bfloat16)],
        compiler_params=PARAMS,
        cost_estimate=cost(2 * big, 3 << 20),
        name="prefix_terms",
    )(meta, queries, grad_output, stats, pairs)

    returned = lax.all_to_all(terms.reshape(near_shape), near, 0, 0, tiled=True)
    summed = pl.pallas_call(
        add_rows,
        in_specs=[smem, vmem],
        out_specs=vmem,
        out_shape=jax.ShapeDtypeStruct(far_shape, jnp.bfloat16),
        scratch_shapes=[pltpu.VMEM(far_shape, jnp.float32)],
        compiler_params=PARAMS,
        name="add_rows",
    )(members, returned)
    owned = lax.all_to_all(summed, far, 0, 0, tiled=True)
    grad_prefix_keys, grad_prefix_values = pl.pallas_call(
        functools.partial(sum_rows, places),
        in_specs=[vmem],
        out_specs=[vmem, vmem],
        out_shape=[jax.ShapeDtypeStruct((1, prefix_rows, HD), jnp.float32)] * 2,
        compiler_params=PARAMS,
        name="sum_rows",
    )(owned)

    grad_queries, grad_keys, grad_values = pl.pallas_call(
        functools.partial(own_grads, dims),
        grid=(steps,),
        in_specs=[smem, heads_q, heads_q, heads_k, heads_k, lanes, parted],
        out_specs=[heads_q, heads_k, heads_k],
        scratch_shapes=[packed, packed, bias],
        out_shape=[
            jax.ShapeDtypeStruct(queries.shape, jnp.bfloat16),
            jax.ShapeDtypeStruct(candidate_keys.shape, jnp.bfloat16),
            jax.ShapeDtypeStruct(candidate_values.shape, jnp.bfloat16),
        ],
        compiler_params=PARAMS,
        cost_estimate=cost(6 * big, 6 << 20),
        name="own_grads",
    )(meta, queries, grad_output, candidate_keys, candidate_values, total, pairs)
    return grad_queries, grad_keys, grad_values, grad_prefix_keys, grad_prefix_values


def solution(mesh, parts=(4, 2, 2, 4)):
    seq = mesh.shape["seq"]
    inner = Mesh(mesh.devices.reshape(parts + (seq,)), ("zh", "zl", "yh", "yl", "seq"))
    dp = ("zh", "zl", "yh", "yl")
    both = dp + ("seq",)
    in_specs = (
        P(both, None, None),
        P(both, None, None),
        P(both, None, None),
        P(both, None, None),
        P(dp, None, "seq"),
        P(dp, None, "seq"),
        P(),
        P(),
        P(),
    )
    out_specs = (
        P(both, None, None),
        P(both, None, None),
        P(both, None, None),
        P(dp, None, "seq"),
        P(dp, None, "seq"),
    )
    return jax.shard_map(local, mesh=inner, in_specs=in_specs, out_specs=out_specs, check_vma=False)
```

```python
import functools
import math

import jax
import jax.numpy as jnp
from jax import lax
from jax.experimental import pallas as pl
from jax.experimental.pallas import tpu as pltpu
from jax.sharding import Mesh, PartitionSpec as P

HD = 128
PAD = 16
NEG = -1e30
VMEM = 24 * 1024 * 1024


def stack_heads(ref, out, part, rows, group, stride):
    for h in range(group):
        lanes = slice((part * group + h) * HD, (part * group + h + 1) * HD)
        out[part, pl.ds(h * stride, rows), :] = ref[0, :, lanes]


def dot_nt(a, b):
    return lax.dot_general(a, b, (((1,), (1,)), ((), ())), preferred_element_type=jnp.float32)


def dot_nn(a, b):
    return lax.dot_general(a, b, (((1,), (0,)), ((), ())), preferred_element_type=jnp.float32)


def dot_tn(a, b):
    return lax.dot_general(a, b, (((0,), (0,)), ((), ())), preferred_element_type=jnp.float32)


def own_bias(bias, length, rows, group, stride):
    inside = lax.broadcasted_iota(jnp.int32, (rows, stride), 0)
    row = lax.broadcasted_iota(jnp.int32, (rows, stride), 1)
    tile = jnp.where(jnp.logical_and(inside <= row, inside < length), 0.0, NEG)
    bias[...] = jnp.concatenate([tile] * group, axis=1)


def own_stats(dims, skips, where, index, lengths, prefixes, q, g, k, v, *refs):
    meta, members, stats, q4, g4, bias = refs
    rows, group, stride, factor, _ = dims

    @pl.when(pl.program_id(0) == 0)
    def _():
        length = lengths[where[1]]
        meta[0] = length
        meta[1] = prefixes[index[where[1]]]
        for i, skip in enumerate(skips):
            members[i] = index[where[0] + skip]
        own_bias(bias, length, rows, group, stride)

    q4[...] = jnp.zeros_like(q4)
    g4[...] = jnp.zeros_like(g4)
    for part in range(q4.shape[0]):
        stack_heads(q, q4, part, rows, group, stride)
        stack_heads(g, g4, part, rows, group, stride)
        lanes = slice(part * HD, (part + 1) * HD)
        scores = dot_nt(k[0, :, lanes], q4[part]) * factor + bias[...]
        highest = jnp.max(scores, axis=0, keepdims=True)
        expon = jnp.exp2(scores - highest)
        grad_probs = dot_nt(v[0, :, lanes], g4[part])
        stats[part, 0:1, :] = highest
        stats[part, 1:2, :] = jnp.sum(expon, axis=0, keepdims=True)
        stats[part, 2:3, :] = jnp.sum(expon * grad_probs, axis=0, keepdims=True)


def live_lanes(length, group, stride):
    row = lax.broadcasted_iota(jnp.int32, (1, stride), 1)
    live = jnp.where(row < length, 1.0, 0.0)
    return jnp.concatenate([live] * group, axis=1)


def prefix_bias(prefix_length, prefix_rows, width):
    column = lax.broadcasted_iota(jnp.int32, (prefix_rows, width), 0)
    return jnp.where(column < prefix_length, 0.0, NEG)


def prefix_terms(dims, meta, q4, g4, stats, pair, total, terms):
    rows, group, stride, factor, scale = dims
    half = pair.shape[0] // 2
    prefix_rows = half * pair.shape[2]

    mask = prefix_bias(meta[1], prefix_rows, group * stride)
    live = live_lanes(meta[0], group, stride)
    for part in range(q4.shape[0]):
        keys = pair[0:half, part].reshape(prefix_rows, HD)
        values = pair[half:, part].reshape(prefix_rows, HD)
        scores = dot_nt(keys, q4[part]) * factor + mask
        own_high = stats[part, 0:1, :]
        highest = jnp.maximum(own_high, jnp.max(scores, axis=0, keepdims=True))
        expon = jnp.exp2(scores - highest)
        fade = jnp.exp2(own_high - highest)
        weight = fade * stats[part, 1:2, :] + jnp.sum(expon, axis=0, keepdims=True)
        inverse = live / weight
        grad_probs = dot_nt(values, g4[part])
        delta = fade * stats[part, 2:3, :] + jnp.sum(expon * grad_probs, axis=0, keepdims=True)
        delta = delta * inverse
        probs = expon * inverse
        grad_scores = (probs * (grad_probs - delta) * scale).astype(jnp.bfloat16)
        total[part, 0:1, :] = highest
        total[part, 1:2, :] = inverse
        total[part, 2:3, :] = delta
        key_terms = dot_nn(grad_scores, q4[part])
        value_terms = dot_nn(probs.astype(jnp.bfloat16), g4[part])
        terms[0:half, part] = key_terms.astype(jnp.bfloat16).reshape((half,) + terms.shape[2:])
        terms[half:, part] = value_terms.astype(jnp.bfloat16).reshape((half,) + terms.shape[2:])


def own_grads(dims, meta, q4, g4, k, v, total, pair, dq, dk, dv, bias):
    rows, group, stride, factor, scale = dims
    half = pair.shape[0] // 2
    prefix_rows = half * pair.shape[2]

    @pl.when(pl.program_id(0) == 0)
    def _():
        own_bias(bias, meta[0], rows, group, stride)

    prefix_mask = prefix_bias(meta[1], prefix_rows, group * stride)
    for part in range(q4.shape[0]):
        highest = total[part, 0:1, :]
        inverse = total[part, 1:2, :]
        delta = total[part, 2:3, :]

        def one(keys, values, mask):
            scores = dot_nt(keys, q4[part]) * factor + mask
            probs = jnp.exp2(scores - highest) * inverse
            grad_probs = dot_nt(values, g4[part])
            return probs, (probs * (grad_probs - delta) * scale).astype(jnp.bfloat16)

        keys = pair[0:half, part].reshape(prefix_rows, HD)
        values = pair[half:, part].reshape(prefix_rows, HD)
        here = slice(part * HD, (part + 1) * HD)
        _, prefix_scores = one(keys, values, prefix_mask)
        probs, grad_scores = one(k[0, :, here], v[0, :, here], bias[...])
        dv[0, :, here] = dot_nn(probs.astype(jnp.bfloat16), g4[part]).astype(jnp.bfloat16)
        dk[0, :, here] = dot_nn(grad_scores, q4[part]).astype(jnp.bfloat16)
        for h in range(group):
            lanes = slice(h * stride, (h + 1) * stride)
            rows_q = dot_tn(grad_scores[:, lanes], k[0, :, here])
            rows_q = rows_q + dot_tn(prefix_scores[:, lanes], keys)
            at = part * group + h
            dq[0, :, at * HD : (at + 1) * HD] = rows_q[:rows].astype(jnp.bfloat16)


def spread(places, keys, values, out, whole):
    prefix_rows = keys.shape[1]
    piece = out.shape[1]
    whole[...] = jnp.zeros_like(whole)
    whole[0:prefix_rows, :] = keys[0]
    middle = whole.shape[0] // 2
    whole[middle : middle + prefix_rows, :] = values[0]
    for i, place in enumerate(places):
        out[i] = whole[place * piece : (place + 1) * piece, :]


def pick_rows(members, source, out):
    for i in range(out.shape[0]):
        out[i] = source[members[i]]


def add_rows(members, source, out, acc):
    acc[...] = jnp.zeros_like(acc)
    for i in range(source.shape[0]):
        at = members[i]
        acc[at] = acc[at] + source[i].astype(jnp.float32)
    out[...] = acc[...].astype(jnp.bfloat16)


PARAMS = pltpu.CompilerParams(vmem_limit_bytes=VMEM)


def streamed(*arrays):
    return tuple(pltpu.with_memory_space_constraint(array, pltpu.HBM) for array in arrays)


def cost(flops, nbytes):
    return pl.CostEstimate(flops=flops, bytes_accessed=nbytes, transcendentals=flops // 256)


def local(
    queries,
    candidate_keys,
    candidate_values,
    grad_output,
    prefix_keys,
    prefix_values,
    query_index,
    candidate_length,
    prefix_length,
):
    far, near, seq = ("zh", "zl", "yh", "yl"), ("zl", "yl", "seq"), "seq"
    rows, width_q = queries.shape[1:]
    kv_heads = candidate_keys.shape[2] // HD
    group = width_q // (kv_heads * HD)
    prefix_rows = prefix_keys.shape[1]
    stride = -(-rows // PAD) * PAD
    width = group * stride
    scale = 1.0 / math.sqrt(HD)
    dims = (rows, group, stride, scale * math.log2(math.e), scale)
    sizes = tuple(lax.axis_size(a) for a in far)
    size_zh, size_zl, size_yh, size_yl = sizes
    size_s = lax.axis_size(seq)
    pieces = size_zl * size_yl
    n_far, n_near = size_zh * size_zl * size_yh * size_yl, pieces * size_s
    half = pieces // 2
    piece = -(-prefix_rows // (half * PAD)) * PAD
    places = tuple(
        ((i // (size_yl * size_yh)) % size_zl) * size_yl + i % size_yl for i in range(n_far)
    )
    skips = tuple(
        (zl * size_yh * size_yl + yl) * size_s + s
        for zl in range(size_zl)
        for yl in range(size_yl)
        for s in range(size_s)
    )
    zh, zl, yh, yl, s = (lax.axis_index(a) for a in far + (seq,))
    first = (zh * size_zl * size_yh + yh) * size_yl * size_s
    mine = first + (zl * size_yh * size_yl + yl) * size_s + s
    where = jnp.stack([first, mine]).astype(jnp.int32)

    smem = pl.BlockSpec(memory_space=pltpu.SMEM)
    vmem = pl.BlockSpec(memory_space=pltpu.VMEM)
    per = 2 if kv_heads % 2 == 0 else 1
    steps = kv_heads // per
    per = 2 if kv_heads % 2 == 0 else 1
    steps = kv_heads // per
    heads_q = pl.BlockSpec((1, rows, per * group * HD), lambda i: (0, 0, i))
    heads_k = pl.BlockSpec((1, rows, per * HD), lambda i: (0, 0, i))
    lanes = pl.BlockSpec((per, 8, width), lambda i: (i, 0, 0))
    parted = pl.BlockSpec((pieces, per, piece, HD), lambda i: (0, i, 0, 0))
    stacked = pl.BlockSpec((per, width, HD), lambda i: (i, 0, 0))
    stacked_shape = jax.ShapeDtypeStruct((kv_heads, width, HD), jnp.bfloat16)
    bias = pltpu.VMEM((rows, width), jnp.float32)
    lane_shape = jax.ShapeDtypeStruct((kv_heads, 8, width), jnp.float32)
    far_shape = (n_far, piece, HD)
    near_shape = (n_near, piece, HD)
    part_shape = (pieces, kv_heads, piece, HD)
    big = kv_heads * width * rows * HD * 2

    everyone = pl.pallas_call(
        functools.partial(spread, places),
        in_specs=[vmem, vmem],
        out_specs=vmem,
        out_shape=jax.ShapeDtypeStruct(far_shape, jnp.bfloat16),
        scratch_shapes=[pltpu.VMEM((pieces * piece, HD), jnp.bfloat16)],
        compiler_params=PARAMS,
        name="spread",
    )(*streamed(prefix_keys, prefix_values))
    held = lax.all_to_all(everyone, far, 0, 0, tiled=True)
    meta, members, stats, stacked_queries, stacked_grads = pl.pallas_call(
        functools.partial(own_stats, dims, skips),
        grid=(steps,),
        in_specs=[smem, smem, smem, smem, heads_q, heads_q, heads_k, heads_k],
        out_specs=[smem, smem, lanes, stacked, stacked],
        scratch_shapes=[bias],
        out_shape=[
            jax.ShapeDtypeStruct((2,), jnp.int32),
            jax.ShapeDtypeStruct((n_near,), jnp.int32),
            lane_shape,
            stacked_shape,
            stacked_shape,
        ],
        compiler_params=PARAMS,
        cost_estimate=cost(2 * big, 3 << 20),
        name="own_stats",
    )(
        where,
        *streamed(
            query_index,
            candidate_length,
            prefix_length,
            queries,
            grad_output,
            candidate_keys,
            candidate_values,
        ),
    )
    chosen = pl.pallas_call(
        pick_rows,
        in_specs=[smem, vmem],
        out_specs=vmem,
        out_shape=jax.ShapeDtypeStruct(near_shape, jnp.bfloat16),
        compiler_params=PARAMS,
        name="pick_rows",
    )(members, held)
    pairs = lax.all_to_all(chosen, near, 0, 0, tiled=True).reshape(part_shape)

    total, terms = pl.pallas_call(
        functools.partial(prefix_terms, dims),
        grid=(steps,),
        in_specs=[smem, stacked, stacked, lanes, parted],
        out_specs=[lanes, parted],
        out_shape=[lane_shape, jax.ShapeDtypeStruct(part_shape, jnp.bfloat16)],
        compiler_params=PARAMS,
        cost_estimate=cost(2 * big, 3 << 20),
        name="prefix_terms",
    )(meta, stacked_queries, stacked_grads, stats, pairs)

    returned = lax.all_to_all(terms.reshape(near_shape), near, 0, 0, tiled=True)
    summed = pl.pallas_call(
        add_rows,
        in_specs=[smem, vmem],
        out_specs=vmem,
        out_shape=jax.ShapeDtypeStruct(far_shape, jnp.bfloat16),
        scratch_shapes=[pltpu.VMEM(far_shape, jnp.float32)],
        compiler_params=PARAMS,
        name="add_rows",
    )(members, returned)
    owned = lax.all_to_all(summed, far, 0, 0, tiled=True)
    owned = owned.reshape(sizes + (piece, HD)).astype(jnp.float32)
    owned = jnp.sum(owned, axis=(0, 2)).reshape(2, half * piece, HD)
    grad_prefix_keys, grad_prefix_values = owned[0:1, :prefix_rows], owned[1:2, :prefix_rows]

    grad_queries, grad_keys, grad_values = pl.pallas_call(
        functools.partial(own_grads, dims),
        grid=(steps,),
        in_specs=[smem, stacked, stacked, heads_k, heads_k, lanes, parted],
        out_specs=[heads_q, heads_k, heads_k],
        scratch_shapes=[bias],
        out_shape=[
            jax.ShapeDtypeStruct(queries.shape, jnp.bfloat16),
            jax.ShapeDtypeStruct(candidate_keys.shape, jnp.bfloat16),
            jax.ShapeDtypeStruct(candidate_values.shape, jnp.bfloat16),
        ],
        compiler_params=PARAMS,
        cost_estimate=cost(6 * big, 6 << 20),
        name="own_grads",
    )(meta, stacked_queries, stacked_grads, candidate_keys, candidate_values, total, pairs)
    return grad_queries, grad_keys, grad_values, grad_prefix_keys, grad_prefix_values


def solution(mesh, parts=(4, 2, 2, 4)):
    seq = mesh.shape["seq"]
    inner = Mesh(mesh.devices.reshape(parts + (seq,)), ("zh", "zl", "yh", "yl", "seq"))
    dp = ("zh", "zl", "yh", "yl")
    both = dp + ("seq",)
    in_specs = (
        P(both, None, None),
        P(both, None, None),
        P(both, None, None),
        P(both, None, None),
        P(dp, None, "seq"),
        P(dp, None, "seq"),
        P(),
        P(),
        P(),
    )
    out_specs = (
        P(both, None, None),
        P(both, None, None),
        P(both, None, None),
        P(dp, None, "seq"),
        P(dp, None, "seq"),
    )
    return jax.shard_map(local, mesh=inner, in_specs=in_specs, out_specs=out_specs, check_vma=False)
```

```python
import functools
import math

import jax
import jax.numpy as jnp
from jax import lax
from jax.experimental import pallas as pl
from jax.experimental.pallas import tpu as pltpu
from jax.sharding import Mesh, PartitionSpec as P

HD = 128
PAD = 16
NEG = -1e30
VMEM = 24 * 1024 * 1024


def stack_heads(ref, out, part, rows, group, stride):
    for h in range(group):
        lanes = slice((part * group + h) * HD, (part * group + h + 1) * HD)
        out[part, pl.ds(h * stride, rows), :] = ref[0, :, lanes]


def dot_nt(a, b):
    return lax.dot_general(a, b, (((1,), (1,)), ((), ())), preferred_element_type=jnp.float32)


def dot_nn(a, b):
    return lax.dot_general(a, b, (((1,), (0,)), ((), ())), preferred_element_type=jnp.float32)


def dot_tn(a, b):
    return lax.dot_general(a, b, (((0,), (0,)), ((), ())), preferred_element_type=jnp.float32)


def own_bias(bias, length, rows, group, stride):
    inside = lax.broadcasted_iota(jnp.int32, (rows, stride), 0)
    row = lax.broadcasted_iota(jnp.int32, (rows, stride), 1)
    tile = jnp.where(jnp.logical_and(inside <= row, inside < length), 0.0, NEG)
    bias[...] = jnp.concatenate([tile] * group, axis=1)


def own_stats(dims, skips, where, index, lengths, prefixes, q, g, k, v, *refs):
    meta, members, stats, q4, g4, bias = refs
    rows, group, stride, factor, _ = dims

    @pl.when(pl.program_id(0) == 0)
    def _():
        length = lengths[where[1]]
        meta[0] = length
        meta[1] = prefixes[index[where[1]]]
        for i, skip in enumerate(skips):
            members[i] = index[where[0] + skip]
        own_bias(bias, length, rows, group, stride)

    q4[...] = jnp.zeros_like(q4)
    g4[...] = jnp.zeros_like(g4)
    for part in range(q4.shape[0]):
        stack_heads(q, q4, part, rows, group, stride)
        stack_heads(g, g4, part, rows, group, stride)
        lanes = slice(part * HD, (part + 1) * HD)
        scores = dot_nt(k[0, :, lanes], q4[part]) * factor + bias[...]
        highest = jnp.max(scores, axis=0, keepdims=True)
        expon = jnp.exp2(scores - highest)
        grad_probs = dot_nt(v[0, :, lanes], g4[part])
        stats[part, 0:1, :] = highest
        stats[part, 1:2, :] = jnp.sum(expon, axis=0, keepdims=True)
        stats[part, 2:3, :] = jnp.sum(expon * grad_probs, axis=0, keepdims=True)


def live_lanes(length, group, stride):
    row = lax.broadcasted_iota(jnp.int32, (1, stride), 1)
    live = jnp.where(row < length, 1.0, 0.0)
    return jnp.concatenate([live] * group, axis=1)


def prefix_bias(prefix_length, prefix_rows, width):
    column = lax.broadcasted_iota(jnp.int32, (prefix_rows, width), 0)
    return jnp.where(column < prefix_length, 0.0, NEG)


def prefix_terms(dims, meta, q4, g4, stats, pair, total, terms):
    rows, group, stride, factor, scale = dims
    half = pair.shape[0] // 2
    prefix_rows = half * pair.shape[2]

    mask = prefix_bias(meta[1], prefix_rows, group * stride)
    live = live_lanes(meta[0], group, stride)
    for part in range(q4.shape[0]):
        keys = pair[0:half, part].reshape(prefix_rows, HD)
        values = pair[half:, part].reshape(prefix_rows, HD)
        scores = dot_nt(keys, q4[part]) * factor + mask
        own_high = stats[part, 0:1, :]
        highest = jnp.maximum(own_high, jnp.max(scores, axis=0, keepdims=True))
        expon = jnp.exp2(scores - highest)
        fade = jnp.exp2(own_high - highest)
        weight = fade * stats[part, 1:2, :] + jnp.sum(expon, axis=0, keepdims=True)
        inverse = live / weight
        grad_probs = dot_nt(values, g4[part])
        delta = fade * stats[part, 2:3, :] + jnp.sum(expon * grad_probs, axis=0, keepdims=True)
        delta = delta * inverse
        probs = expon * inverse
        grad_scores = (probs * (grad_probs - delta) * scale).astype(jnp.bfloat16)
        total[part, 0:1, :] = highest
        total[part, 1:2, :] = inverse
        total[part, 2:3, :] = delta
        key_terms = dot_nn(grad_scores, q4[part])
        value_terms = dot_nn(probs.astype(jnp.bfloat16), g4[part])
        terms[0:half, part] = key_terms.astype(jnp.bfloat16).reshape((half,) + terms.shape[2:])
        terms[half:, part] = value_terms.astype(jnp.bfloat16).reshape((half,) + terms.shape[2:])


def own_grads(dims, meta, q4, g4, k, v, total, pair, dq, dk, dv, bias):
    rows, group, stride, factor, scale = dims
    half = pair.shape[0] // 2
    prefix_rows = half * pair.shape[2]

    @pl.when(pl.program_id(0) == 0)
    def _():
        own_bias(bias, meta[0], rows, group, stride)

    prefix_mask = prefix_bias(meta[1], prefix_rows, group * stride)
    for part in range(q4.shape[0]):
        highest = total[part, 0:1, :]
        inverse = total[part, 1:2, :]
        delta = total[part, 2:3, :]

        def one(keys, values, mask):
            scores = dot_nt(keys, q4[part]) * factor + mask
            probs = jnp.exp2(scores - highest) * inverse
            grad_probs = dot_nt(values, g4[part])
            return probs, (probs * (grad_probs - delta) * scale).astype(jnp.bfloat16)

        keys = pair[0:half, part].reshape(prefix_rows, HD)
        values = pair[half:, part].reshape(prefix_rows, HD)
        here = slice(part * HD, (part + 1) * HD)
        _, prefix_scores = one(keys, values, prefix_mask)
        probs, grad_scores = one(k[0, :, here], v[0, :, here], bias[...])
        dv[0, :, here] = dot_nn(probs.astype(jnp.bfloat16), g4[part]).astype(jnp.bfloat16)
        dk[0, :, here] = dot_nn(grad_scores, q4[part]).astype(jnp.bfloat16)
        for h in range(group):
            lanes = slice(h * stride, (h + 1) * stride)
            rows_q = dot_tn(grad_scores[:, lanes], k[0, :, here])
            rows_q = rows_q + dot_tn(prefix_scores[:, lanes], keys)
            at = part * group + h
            dq[0, :, at * HD : (at + 1) * HD] = rows_q[:rows].astype(jnp.bfloat16)


def spread(places, keys, values, out, whole):
    prefix_rows = keys.shape[1]
    piece = out.shape[1]
    whole[...] = jnp.zeros_like(whole)
    whole[0:prefix_rows, :] = keys[0]
    middle = whole.shape[0] // 2
    whole[middle : middle + prefix_rows, :] = values[0]
    for i, place in enumerate(places):
        out[i] = whole[place * piece : (place + 1) * piece, :]


def pick_rows(members, source, out):
    for i in range(out.shape[0]):
        out[i] = source[members[i]]


def add_rows(members, source, out, acc):
    acc[...] = jnp.zeros_like(acc)
    for i in range(source.shape[0]):
        at = members[i]
        acc[at] = acc[at] + source[i].astype(jnp.float32)
    out[...] = acc[...].astype(jnp.bfloat16)


PARAMS = pltpu.CompilerParams(vmem_limit_bytes=VMEM)


def streamed(*arrays):
    return tuple(pltpu.with_memory_space_constraint(array, pltpu.HBM) for array in arrays)


def cost(flops, nbytes):
    return pl.CostEstimate(flops=flops, bytes_accessed=nbytes, transcendentals=flops // 256)


def local(
    queries,
    candidate_keys,
    candidate_values,
    grad_output,
    prefix_keys,
    prefix_values,
    query_index,
    candidate_length,
    prefix_length,
):
    far, near, seq = ("zh", "zl", "yh", "yl"), ("zl", "yl", "seq"), "seq"
    rows, width_q = queries.shape[1:]
    kv_heads = candidate_keys.shape[2] // HD
    group = width_q // (kv_heads * HD)
    prefix_rows = prefix_keys.shape[1]
    stride = -(-rows // PAD) * PAD
    width = group * stride
    scale = 1.0 / math.sqrt(HD)
    dims = (rows, group, stride, scale * math.log2(math.e), scale)
    sizes = tuple(lax.axis_size(a) for a in far)
    size_zh, size_zl, size_yh, size_yl = sizes
    size_s = lax.axis_size(seq)
    pieces = size_zl * size_yl
    n_far, n_near = size_zh * size_zl * size_yh * size_yl, pieces * size_s
    half = pieces // 2
    piece = -(-prefix_rows // (half * PAD)) * PAD
    places = tuple(
        ((i // (size_yl * size_yh)) % size_zl) * size_yl + i % size_yl for i in range(n_far)
    )
    skips = tuple(
        (zl * size_yh * size_yl + yl) * size_s + s
        for zl in range(size_zl)
        for yl in range(size_yl)
        for s in range(size_s)
    )
    zh, zl, yh, yl, s = (lax.axis_index(a) for a in far + (seq,))
    first = (zh * size_zl * size_yh + yh) * size_yl * size_s
    mine = first + (zl * size_yh * size_yl + yl) * size_s + s
    where = jnp.stack([first, mine]).astype(jnp.int32)

    smem = pl.BlockSpec(memory_space=pltpu.SMEM)
    vmem = pl.BlockSpec(memory_space=pltpu.VMEM)
    per = 2 if kv_heads % 2 == 0 else 1
    steps = kv_heads // per
    per = 2 if kv_heads % 2 == 0 else 1
    steps = kv_heads // per
    heads_q = pl.BlockSpec((1, rows, per * group * HD), lambda i: (0, 0, i))
    heads_k = pl.BlockSpec((1, rows, per * HD), lambda i: (0, 0, i))
    lanes = pl.BlockSpec((per, 8, width), lambda i: (i, 0, 0))
    parted = pl.BlockSpec((pieces, per, piece, HD), lambda i: (0, i, 0, 0))
    stacked = pl.BlockSpec((per, width, HD), lambda i: (i, 0, 0))
    stacked_shape = jax.ShapeDtypeStruct((kv_heads, width, HD), jnp.bfloat16)
    bias = pltpu.VMEM((rows, width), jnp.float32)
    lane_shape = jax.ShapeDtypeStruct((kv_heads, 8, width), jnp.float32)
    far_shape = (n_far, piece, HD)
    near_shape = (n_near, piece, HD)
    part_shape = (pieces, kv_heads, piece, HD)
    big = kv_heads * width * rows * HD * 2

    everyone = pl.pallas_call(
        functools.partial(spread, places),
        in_specs=[vmem, vmem],
        out_specs=vmem,
        out_shape=jax.ShapeDtypeStruct(far_shape, jnp.bfloat16),
        scratch_shapes=[pltpu.VMEM((pieces * piece, HD), jnp.bfloat16)],
        compiler_params=PARAMS,
        name="spread",
    )(*streamed(prefix_keys, prefix_values))
    held = lax.all_to_all(everyone, far, 0, 0, tiled=True)
    meta, members, stats, stacked_queries, stacked_grads = pl.pallas_call(
        functools.partial(own_stats, dims, skips),
        grid=(steps,),
        in_specs=[smem, smem, smem, smem, heads_q, heads_q, heads_k, heads_k],
        out_specs=[smem, smem, lanes, stacked, stacked],
        scratch_shapes=[bias],
        out_shape=[
            jax.ShapeDtypeStruct((2,), jnp.int32),
            jax.ShapeDtypeStruct((n_near,), jnp.int32),
            lane_shape,
            stacked_shape,
            stacked_shape,
        ],
        compiler_params=PARAMS,
        cost_estimate=cost(2 * big, 3 << 20),
        name="own_stats",
    )(
        where,
        *streamed(
            query_index,
            candidate_length,
            prefix_length,
            queries,
            grad_output,
            candidate_keys,
            candidate_values,
        ),
    )
    chosen = pl.pallas_call(
        pick_rows,
        in_specs=[smem, vmem],
        out_specs=vmem,
        out_shape=jax.ShapeDtypeStruct(near_shape, jnp.bfloat16),
        compiler_params=PARAMS,
        name="pick_rows",
    )(members, held)
    pairs = lax.all_to_all(chosen, near, 0, 0, tiled=True).reshape(part_shape)

    total, terms = pl.pallas_call(
        functools.partial(prefix_terms, dims),
        in_specs=[smem, vmem, vmem, vmem, vmem],
        out_specs=[vmem, vmem],
        out_shape=[lane_shape, jax.ShapeDtypeStruct(part_shape, jnp.bfloat16)],
        compiler_params=PARAMS,
        cost_estimate=cost(2 * big, 3 << 20),
        name="prefix_terms",
    )(meta, stacked_queries, stacked_grads, stats, pairs)

    returned = lax.all_to_all(terms.reshape(near_shape), near, 0, 0, tiled=True)
    summed = pl.pallas_call(
        add_rows,
        in_specs=[smem, vmem],
        out_specs=vmem,
        out_shape=jax.ShapeDtypeStruct(far_shape, jnp.bfloat16),
        scratch_shapes=[pltpu.VMEM(far_shape, jnp.float32)],
        compiler_params=PARAMS,
        name="add_rows",
    )(members, returned)
    owned = lax.all_to_all(summed, far, 0, 0, tiled=True)
    owned = owned.reshape(sizes + (piece, HD)).astype(jnp.float32)
    owned = jnp.sum(owned, axis=(0, 2)).reshape(2, half * piece, HD)
    grad_prefix_keys, grad_prefix_values = owned[0:1, :prefix_rows], owned[1:2, :prefix_rows]

    grad_queries, grad_keys, grad_values = pl.pallas_call(
        functools.partial(own_grads, dims),
        grid=(steps,),
        in_specs=[smem, stacked, stacked, heads_k, heads_k, lanes, parted],
        out_specs=[heads_q, heads_k, heads_k],
        scratch_shapes=[bias],
        out_shape=[
            jax.ShapeDtypeStruct(queries.shape, jnp.bfloat16),
            jax.ShapeDtypeStruct(candidate_keys.shape, jnp.bfloat16),
            jax.ShapeDtypeStruct(candidate_values.shape, jnp.bfloat16),
        ],
        compiler_params=PARAMS,
        cost_estimate=cost(6 * big, 6 << 20),
        name="own_grads",
    )(
        meta,
        stacked_queries,
        stacked_grads,
        *streamed(candidate_keys, candidate_values),
        total,
        pairs,
    )
    return grad_queries, grad_keys, grad_values, grad_prefix_keys, grad_prefix_values


def solution(mesh, parts=(4, 2, 2, 4)):
    seq = mesh.shape["seq"]
    inner = Mesh(mesh.devices.reshape(parts + (seq,)), ("zh", "zl", "yh", "yl", "seq"))
    dp = ("zh", "zl", "yh", "yl")
    both = dp + ("seq",)
    in_specs = (
        P(both, None, None),
        P(both, None, None),
        P(both, None, None),
        P(both, None, None),
        P(dp, None, "seq"),
        P(dp, None, "seq"),
        P(),
        P(),
        P(),
    )
    out_specs = (
        P(both, None, None),
        P(both, None, None),
        P(both, None, None),
        P(dp, None, "seq"),
        P(dp, None, "seq"),
    )
    return jax.shard_map(local, mesh=inner, in_specs=in_specs, out_specs=out_specs, check_vma=False)
```
